256 devices in a mesh: rows: 64 (over y, z, core), rep: 4 (over x).
Axes of the slice: x: 4, y: 4, z: 8, core: 2. Of those that a mesh axis runs over, the one named last changes fastest.
Arguments:
- tiles: bfloat16 [64, 4, 32, 256, 256], P('rows', 'rep'), may hold values from -6 to 6
- tile_row: int32 [64, 4, 32], P('rows', 'rep'), may hold values from 0 to 3
- tile_col: int32 [64, 4, 32], P('rows', 'rep'), may hold values from 0 to 3
- tile_round: int32 [64, 4, 32], P('rows', 'rep'), may hold values from 0 to 4
- tile_count: int32 [64, 4], P('rows', 'rep'), may hold values from 8 to 32, as said below
- start_block: float32 [32, 65536], P(None, ('rows', 'rep')), may hold values from -6 to 6
Outputs:
- next_block: float32 [32, 65536], P(None, ('rows', 'rep'))
- coefficients: float32 [2, 64, 32], replicated
- factors: float32 [2, 32, 32], replicated
The draws below stay inside these ranges and needn't reach their ends.
Inputs may be any that keep to these rules, and one draw needn't show every extreme that they name: `tile_count`: slots at or above a device's count hold entries that are not part of the matrix; in every draw some device has count 32 and some has the least count.
All inputs are finite; a program needn't handle non-finite values.
Results may differ from the reference program's by a relative error of at most 0.0041.
Values may be sent and summed in bfloat16 or wider, within the bound.
No kernel may reach another device: no remote copies, remote signals or barrier semaphores. Data moves between devices by JAX's collectives and lax.ppermute only.
A program may use at most 64 MiB of HBM per device.

```python
import math
import jax
import jax.numpy as jnp
from jax import lax

K = 32
BS = 256
BLK_DEV = 4
SLOTS = 32
ROUNDS = 4
ITERS = 2
NODES = 65536
N_ROWS = 64
N_REP = 4


def draw_tiles(key, part):
    key = jax.random.fold_in(key, 11)
    normal_key, level_key = jax.random.split(key)
    tile_shape = (N_ROWS, N_REP, SLOTS, BS, BS)
    entry_scale = 1.0 / math.sqrt(BS)
    spread = jnp.clip(jax.random.normal(normal_key, tile_shape, jnp.float32), -5.0, 5.0) * entry_scale
    level_low = 0.5
    diag_level = jnp.exp(jax.random.uniform(level_key, (N_ROWS, N_REP, SLOTS, BS), jnp.float32, math.log(level_low), math.log(2.0)))
    rise_factor = 1.0 + 2.0 * jnp.arange(N_ROWS, dtype=jnp.float32) / max(N_ROWS - 1, 1)
    diag_level = diag_level * rise_factor[:, None, None, None]
    on_diagonal = lax.iota(jnp.int32, BS)[:, None] == lax.iota(jnp.int32, BS)[None, :]
    return jnp.where(on_diagonal, diag_level[..., None], spread).astype(jnp.bfloat16)


def draw_tile_count(key, part):
    key = jax.random.fold_in(key, 23)
    count_key, order_key = jax.random.split(key)
    least_count = max(1, SLOTS // 4)
    counts = jax.random.randint(count_key, (N_ROWS * N_REP,), least_count, SLOTS + 1, dtype=jnp.int32)
    chosen_order = jax.random.permutation(order_key, N_ROWS * N_REP)
    positions = jnp.arange(N_ROWS * N_REP, dtype=jnp.int32)
    counts = jnp.where(positions == chosen_order[0], SLOTS, jnp.where(positions == chosen_order[1], least_count, counts))
    return counts.reshape(N_ROWS, N_REP).astype(jnp.int32)


def with_ends(values, key, smallest, high):
    longest = values.shape.index(max(values.shape))
    spots = []
    for shift in (0, 1):
        where = [jax.random.randint(jax.random.fold_in(key, axis), (), 0, length) for axis, length in enumerate(values.shape)]
        where[longest] = (where[longest] + shift) % values.shape[longest]
        spots.append(tuple(where))
    return values.at[spots[0]].set(smallest).at[spots[1]].set(high)


def shard_levels(rng, shape, cuts, low, top_value):
    def one(dim, blocks):
        heights = jax.random.uniform(jax.random.fold_in(jax.random.fold_in(rng, 6), dim), (blocks,), jnp.float32, low / len(cuts), top_value / len(cuts))
        return jnp.repeat(jnp.exp(heights), shape[dim] // blocks).reshape((-1,) + (1,) * (len(shape) - dim - 1))

    level = one(*cuts[0])
    for cut in cuts[1:]:
        level = level * one(*cut)
    return level


def scatter_about(rng, shape, scale, bound, cuts=(), held_as=jnp.bfloat16):
    entries = scale * jax.random.normal(rng, shape, jnp.float32)
    if cuts:
        entries = entries * shard_levels(rng, shape, cuts, -0.22, 0.18)
    return jnp.clip(entries, -bound, bound).astype(held_as)


def setup_inputs(seed: int = 0) -> dict:
    keys = jax.random.split(jax.random.key(seed), 7)
    return {
        "tiles": draw_tiles(jax.random.fold_in(keys[6], 71), 0),
        "tile_row": with_ends(jax.random.randint(keys[1], (N_ROWS, N_REP, SLOTS), 0, BLK_DEV), jax.random.fold_in(keys[1], 1), 0, BLK_DEV - 1).astype(jnp.int32),
        "tile_col": with_ends(jax.random.randint(keys[2], (N_ROWS, N_REP, SLOTS), 0, BLK_DEV), jax.random.fold_in(keys[2], 1), 0, BLK_DEV - 1).astype(jnp.int32),
        "tile_round": with_ends(jax.random.randint(keys[3], (N_ROWS, N_REP, SLOTS), 0, ROUNDS + 1), jax.random.fold_in(keys[3], 1), 0, ROUNDS).astype(jnp.int32),
        "tile_count": draw_tile_count(jax.random.fold_in(keys[6], 71), 0),
        "start_block": scatter_about(keys[5], (K, NODES), 1.0, 6.0, ((1, 256),), jnp.float32),
    }


def offsets_table():
    return jnp.array([0] + [max(1, N_ROWS // 2 ** round_index) for round_index in range(1, ROUNDS + 1)], dtype=jnp.int32)

def apply_operator(basis_bf, tiles, tile_row, tile_col, tile_round, tile_count):
    blocks = basis_bf.reshape(K, N_ROWS, BLK_DEV, BS)
    shifts = offsets_table()
    slot_ids = jnp.arange(SLOTS, dtype=jnp.int32)
    block_ids = jnp.arange(BLK_DEV, dtype=jnp.int32)
    target_ids = jnp.arange((ROUNDS + 1) * BLK_DEV, dtype=jnp.int32)

    def holder(flat_index):
        device = flat_index // N_REP
        member = flat_index % N_REP
        tile_mats = tiles[device, member].astype(jnp.float32)
        tile_rows = tile_row[device, member]
        tile_cols = tile_col[device, member]
        tile_rounds = tile_round[device, member]
        live_mask = (slot_ids < tile_count[device, member]).astype(jnp.float32)
        partner = (device + shifts[tile_rounds]) % N_ROWS
        inputs = blocks[:, partner, tile_cols].astype(jnp.float32)
        own_blocks = blocks[:, device, tile_rows].astype(jnp.float32)
        forward = jnp.einsum('ktj,tij->tki', inputs, tile_mats)
        backward = jnp.einsum('kti,tij->tkj', own_blocks, tile_mats)
        pick_row = (tile_rows[:, None] == block_ids[None, :]).astype(jnp.float32) * live_mask[:, None]
        pick_dest = ((tile_rounds * BLK_DEV + tile_cols)[:, None] == target_ids[None, :]).astype(jnp.float32) * live_mask[:, None]
        own_sum = jnp.einsum('tb,tki->kbi', pick_row, forward, precision=lax.Precision.HIGHEST)
        targets = jnp.einsum('tc,tkj->kcj', pick_dest, backward, precision=lax.Precision.HIGHEST)
        kept_sum = own_sum + targets[:, :BLK_DEV]
        sent_sum = targets[:, BLK_DEV:].astype(jnp.bfloat16)
        return (kept_sum, sent_sum)
    kept_sum, sent_sum = lax.map(holder, jnp.arange(N_ROWS * N_REP, dtype=jnp.int32))
    kept_sum = kept_sum.reshape(N_ROWS, N_REP, K, BLK_DEV, BS).sum(axis=1)
    sent_sum = sent_sum.astype(jnp.float32).reshape(N_ROWS, N_REP, K, ROUNDS, BLK_DEV, BS).sum(axis=1)
    total_sum = kept_sum
    for round_index in range(1, ROUNDS + 1):
        total_sum = total_sum + jnp.roll(sent_sum[:, :, round_index - 1], max(1, N_ROWS // 2 ** round_index), axis=0)
    return jnp.transpose(total_sum, (1, 0, 2, 3)).reshape(K, NODES)

def orthonormal(block_now):
    gram_matrix = jnp.dot(block_now, block_now.T, precision=lax.Precision.HIGHEST)
    lower_factor = jnp.linalg.cholesky(gram_matrix)
    solved = jax.scipy.linalg.solve_triangular(lower_factor, block_now, lower=True)
    return (solved, lower_factor)

def reference(tiles, tile_row, tile_col, tile_round, tile_count, start_block):
    basis_now, first_factor = orthonormal(start_block)
    previous = jnp.zeros_like(basis_now)
    coefficient_list = []
    factor_list = []
    for iteration in range(ITERS):
        image_block = apply_operator(basis_now.astype(jnp.bfloat16), tiles, tile_row, tile_col, tile_round, tile_count)
        stacked_basis = jnp.concatenate([basis_now, previous], axis=0)
        coefficient = jnp.dot(stacked_basis, image_block.T, precision=lax.Precision.HIGHEST)
        residue = image_block - jnp.dot(coefficient.T, stacked_basis, precision=lax.Precision.HIGHEST)
        new_basis, lower_factor = orthonormal(residue)
        coefficient_list.append(coefficient)
        factor_list.append(lower_factor)
        previous = basis_now
        basis_now = new_basis
    return (basis_now, jnp.stack(coefficient_list, 0), jnp.stack(factor_list, 0))
```

```python
import functools

import jax
import jax.numpy as jnp
from jax import lax
from jax.experimental import pallas as pl
from jax.experimental.pallas import tpu as pltpu
from jax.sharding import PartitionSpec as P

ROUNDS = 4
F32 = jnp.float32
BF16 = jnp.bfloat16
HIGHEST = lax.Precision.HIGHEST
CHUNK = 4
VMEM_LIMIT = 40 * 1024 * 1024


def dot(a, b, dims, precision=None):
    return lax.dot_general(a, b, (dims, ((), ())), precision=precision, preferred_element_type=F32)


NN = ((1,), (0,))
NT = ((1,), (1,))
TN = ((0,), (0,))


def split(x):
    high = x.astype(BF16)
    low = (x - high.astype(F32)).astype(BF16)
    return jnp.concatenate([high, low], axis=0)


def tile_copies(tiles_ref, held, sems):
    copies = []
    for i in range(held.shape[0] // CHUNK):
        part = pl.ds(i * CHUNK, CHUNK)
        copies.append(pltpu.make_async_copy(tiles_ref.at[part], held.at[part], sems.at[i]))
    return copies


def backward_kernel(row, col, rnd, count, tiles_ref, q_ref, *rest):
    outs, (held, terms, total, sems) = rest[:-4], rest[-4:]
    blocks = q_ref.shape[0]
    trash = total.shape[0] - 1
    copies = tile_copies(tiles_ref, held, sems)
    for copy in copies:
        copy.start()
    member = lax.axis_index("rep")
    for b in range(blocks):
        terms[b] = split(q_ref[b])
    total[...] = jnp.zeros_like(total)
    for t in range(held.shape[0]):
        if t % CHUNK == 0:
            copies[t // CHUNK].wait()
        source = lax.rem(member - row[t] + blocks, blocks)
        target = rnd[t] * blocks + lax.rem(member - col[t] + blocks, blocks)
        target = jnp.where(t < count[0], target, trash)
        product = dot(terms[source], held[t], NN)
        half = product.shape[0] // 2
        total[target] += product[:half] + product[half:]
    for i, out in enumerate(outs):
        out[...] = total[i * blocks : (i + 1) * blocks]


def forward_kernel(row, col, rnd, count, tiles_ref, kept_ref, *rest):
    sources, out, (held, terms, total, sems) = rest[: ROUNDS + 1], rest[ROUNDS + 1], rest[-4:]
    blocks = kept_ref.shape[0]
    trash = blocks
    copies = tile_copies(tiles_ref, held, sems)
    for copy in copies:
        copy.start()
    member = lax.axis_index("rep")
    for i, ref in enumerate(sources):
        for b in range(blocks):
            terms[i * blocks + b] = split(ref[b])
    total[:blocks] = kept_ref[...]
    total[trash] = jnp.zeros(total.shape[1:], F32)
    for t in range(held.shape[0]):
        if t % CHUNK == 0:
            copies[t // CHUNK].wait()
        source = rnd[t] * blocks + lax.rem(member - col[t] + blocks, blocks)
        target = lax.rem(member - row[t] + blocks, blocks)
        target = jnp.where(t < count[0], target, trash)
        product = dot(terms[source], held[t], NT)
        half = product.shape[0] // 2
        total[target] += product[:half] + product[half:]
    out[...] = total[:blocks]


def gram_kernel(s_ref, y_ref, z_ref, out):
    blocks, k, width = s_ref.shape
    grams = []
    for b in range(blocks):
        stack = jnp.concatenate([s_ref[b], y_ref[b], z_ref[b], jnp.zeros((k, width), F32)], axis=0)
        grams.append(dot(stack[: 3 * k], stack, NT, HIGHEST))
    half = blocks // 2
    pairs = [grams[i] + grams[i + half] for i in range(half)]
    out[...] = functools.reduce(lambda a, b: a + b, pairs)


def tail_kernel(gram_ref, s_ref, y_ref, z_ref, next_ref, coef_ref, fact_ref, upper, inverse):
    n, lanes = gram_ref.shape
    k = n // 3
    rows8 = 8
    tiles = n // rows8
    lane = lax.broadcasted_iota(jnp.int32, (rows8, lanes), 1)
    sub = lax.broadcasted_iota(jnp.int32, (rows8, lanes), 0)
    left = [gram_ref[i * rows8 : (i + 1) * rows8, :] for i in range(tiles)]
    right = [jnp.where(lane == sub + i * rows8, 1.0, 0.0).astype(F32) for i in range(tiles)]
    for step in range(n):
        j, r = divmod(step, rows8)
        row_left = left[j][r : r + 1, :]
        row_right = right[j][r : r + 1, :]
        pivot = row_left[:, step : step + 1]
        scale = 1.0 / pivot
        scaled_left = row_left * scale
        scaled_right = row_right * scale
        for i in range(j, tiles):
            factor = left[i][:, step : step + 1]
            if i == j:
                factor = jnp.where(sub[:, :1] > r, factor, 0.0)
            left[i] = left[i] - factor * scaled_left
            right[i] = right[i] - factor * scaled_right
        root = lax.rsqrt(pivot)
        upper[step : step + 1, :] = row_left * root
        inverse[step : step + 1, :] = row_right * root
    u11 = upper[:k, :]
    x = inverse[...]
    u = upper[...]
    u12, u13 = u[:k, k : 2 * k], u[:k, 2 * k : 3 * k]
    u22, u23 = u[k : 2 * k, k : 2 * k], u[k : 2 * k, 2 * k : 3 * k]
    u33 = u[2 * k : 3 * k, 2 * k : 3 * k]
    x11, x22 = x[:k, :k], x[k : 2 * k, k : 2 * k]
    fact_ref[0] = dot(x11, u22, NT, HIGHEST)
    fact_ref[1] = dot(x22, u33, NT, HIGHEST)
    coef_ref[0, :k] = dot(u12, x11, NT, HIGHEST)
    coef_ref[0, k:] = jnp.zeros((k, k), F32)
    v = dot(x11, u12, TN, HIGHEST)
    coef_ref[1, :k] = dot(u23 - dot(u22, v, NN, HIGHEST), x22, NT, HIGHEST)
    coef_ref[1, k:] = dot(u13 - dot(u12, v, NN, HIGHEST), x22, NT, HIGHEST)
    last = x[2 * k : 3 * k, : 3 * k]
    stack = jnp.concatenate([s_ref[0], y_ref[0], z_ref[0]], axis=0)
    next_ref[...] = dot(last, stack, NN, HIGHEST)


def moved(x, axis, target):
    size = lax.axis_size(axis)
    return lax.ppermute(x, axis, [(i, target(i) % size) for i in range(size)])


def shifted(x, axis, by):
    return moved(x, axis, lambda i: i + by)


def sum_of_ring(x, ring):
    first, second, third = ring(1), ring(2), ring(3)
    return (x + second) + (first + third)


def body(tiles, tile_row, tile_col, tile_round, tile_count, start_block):
    tiles = tiles[0, 0]
    meta = (tile_row[0, 0], tile_col[0, 0], tile_round[0, 0], tile_count[0])
    slots, edge = tiles.shape[0], tiles.shape[1]
    k = start_block.shape[0]
    members = lax.axis_size("rep")
    devices = lax.axis_size("rows")
    blocks = members
    offsets = [max(1, devices // 2**r) for r in range(1, ROUNDS + 1)]
    held_shape = (blocks, k, edge)
    smem = pl.BlockSpec(memory_space=pltpu.SMEM)
    vmem = pl.BlockSpec(memory_space=pltpu.VMEM)
    hbm = pl.BlockSpec(memory_space=pl.ANY)
    block_shape = jax.ShapeDtypeStruct(held_shape, F32)
    params = pltpu.CompilerParams(vmem_limit_bytes=VMEM_LIMIT)
    cost = pl.CostEstimate(
        flops=4 * slots * edge * edge * k, bytes_accessed=2 * slots * edge * edge, transcendentals=0
    )

    def scratch(sources, targets):
        return [
            pltpu.VMEM((slots, edge, edge), BF16),
            pltpu.VMEM((sources, 2 * k, edge), BF16),
            pltpu.VMEM((targets + 1, k, edge), F32),
            pltpu.SemaphoreType.DMA((slots // CHUNK,)),
        ]

    backward = pl.pallas_call(
        backward_kernel,
        out_shape=[block_shape] * (ROUNDS + 1),
        in_specs=[smem] * 4 + [hbm, vmem],
        out_specs=[vmem] * (ROUNDS + 1),
        scratch_shapes=scratch(blocks, (ROUNDS + 1) * blocks),
        compiler_params=params,
        cost_estimate=cost,
    )
    forward = pl.pallas_call(
        forward_kernel,
        out_shape=block_shape,
        in_specs=[smem] * 4 + [hbm] + [vmem] * (ROUNDS + 2),
        out_specs=vmem,
        scratch_shapes=scratch((ROUNDS + 1) * blocks, blocks),
        compiler_params=params,
        cost_estimate=cost,
    )

    def rep_sum(part):
        return sum_of_ring(part, lambda by: jnp.roll(shifted(part, "rep", by), by, axis=0))

    def apply(q):
        sources = [shifted(q, "rows", -offset) for offset in offsets]
        kept, *outgoing = backward(*meta, tiles, q)
        arrived = [shifted(x, "rows", offset) for x, offset in zip(outgoing, offsets)]
        part = forward(*meta, tiles, kept, q, *sources)
        for x in arrived:
            part = part + x
        return rep_sum(part)

    start = jnp.stack([start_block] + [shifted(start_block, "rep", by) for by in range(1, members)], 0)
    first = apply(start)
    second = apply(first)
    gram = pl.pallas_call(
        gram_kernel,
        out_shape=jax.ShapeDtypeStruct((3 * k, 4 * k), F32),
        in_specs=[vmem] * 3,
        out_specs=vmem,
        compiler_params=params,
    )(start, first, second)
    gram = gram + moved(gram, "rows", lambda i: i ^ 1)
    gram = sum_of_ring(gram, lambda by: shifted(gram, "rows", by * (devices // 4)))
    gram = gram + moved(gram, "rows", lambda i: i ^ 8)
    gram = sum_of_ring(gram, lambda by: moved(gram, "rows", lambda i: (i & ~7) | ((i + 2 * by) & 7)))
    result, coefficients, factors = pl.pallas_call(
        tail_kernel,
        out_shape=[
            jax.ShapeDtypeStruct((k, edge), F32),
            jax.ShapeDtypeStruct((2, 2 * k, k), F32),
            jax.ShapeDtypeStruct((2, k, k), F32),
        ],
        in_specs=[vmem] * 4,
        out_specs=[vmem] * 3,
        scratch_shapes=[pltpu.VMEM((3 * k, 4 * k), F32), pltpu.VMEM((3 * k, 4 * k), F32)],
        compiler_params=params,
    )(gram, start, first, second)
    return result, coefficients, factors


def solution(mesh):
    placed = (
        P("rows", "rep", None, None, None),
        P("rows", "rep", None),
        P("rows", "rep", None),
        P("rows", "rep", None),
        P("rows", "rep"),
        P(None, ("rows", "rep")),
    )
    return jax.shard_map(
        body,
        mesh=mesh,
        in_specs=placed,
        out_specs=(P(None, ("rows", "rep")), P(), P()),
        check_vma=False,
    )
```

```python
import functools

import jax
import jax.numpy as jnp
from jax import lax
from jax.experimental import pallas as pl
from jax.experimental.pallas import tpu as pltpu
from jax.sharding import PartitionSpec as P

ROUNDS = 4
F32 = jnp.float32
BF16 = jnp.bfloat16
HIGHEST = lax.Precision.HIGHEST
VMEM_LIMIT = 40 * 1024 * 1024


def dot(a, b, dims, precision=None):
    return lax.dot_general(a, b, (dims, ((), ())), precision=precision, preferred_element_type=F32)


NN = ((1,), (0,))
NT = ((1,), (1,))
TN = ((0,), (0,))


def split(x):
    high = x.astype(BF16)
    low = (x - high.astype(F32)).astype(BF16)
    return jnp.concatenate([high, low], axis=0)


def stage_kernel(row_in, col_in, rnd_in, count_in, tiles_ref, held, meta, row, col, rnd, count, sems):
    pairs = [(tiles_ref, held), (row_in, row), (col_in, col), (rnd_in, rnd), (count_in, count)]
    copies = [pltpu.make_async_copy(a, b, sems.at[i]) for i, (a, b) in enumerate(pairs)]
    for copy in copies:
        copy.start()
    member = lax.axis_index("rep")
    blocks = lax.axis_size("rep")
    for copy in copies[1:]:
        copy.wait()
    for t in range(held.shape[0]):
        meta[0, t] = rnd[0, 0, t] * blocks + lax.rem(member - col[0, 0, t] + blocks, blocks)
        meta[1, t] = lax.rem(member - row[0, 0, t] + blocks, blocks)
        meta[2, t] = jnp.where(t < count[0, 0], 1, 0)
    copies[0].wait()


def backward_kernel(meta, held, q_ref, *rest):
    outs, (terms, total) = rest[:-2], rest[-2:]
    blocks = q_ref.shape[0]
    trash = total.shape[0] - 1
    for b in range(blocks):
        terms[b] = split(q_ref[b])
    total[...] = jnp.zeros_like(total)
    for t in range(held.shape[0]):
        source = meta[1, t]
        target = jnp.where(meta[2, t] > 0, meta[0, t], trash)
        product = dot(terms[source], held[t], NN)
        half = product.shape[0] // 2
        total[target] += product[:half] + product[half:]
    for i, out in enumerate(outs):
        out[...] = total[i * blocks : (i + 1) * blocks]


def forward_kernel(meta, held, kept_ref, *rest):
    sources, out, (terms, total) = rest[: ROUNDS + 1], rest[ROUNDS + 1], rest[-2:]
    blocks = kept_ref.shape[0]
    trash = blocks
    for i, ref in enumerate(sources):
        for b in range(blocks):
            terms[i * blocks + b] = split(ref[b])
    total[:blocks] = kept_ref[...]
    total[trash] = jnp.zeros(total.shape[1:], F32)
    for t in range(held.shape[0]):
        source = meta[0, t]
        target = jnp.where(meta[2, t] > 0, meta[1, t], trash)
        product = dot(terms[source], held[t], NT)
        half = product.shape[0] // 2
        total[target] += product[:half] + product[half:]
    out[...] = total[:blocks]


def gram_kernel(s_ref, y_ref, z_ref, out):
    blocks, k, width = s_ref.shape
    grams = []
    for b in range(blocks):
        stack = jnp.concatenate([s_ref[b], y_ref[b], z_ref[b], jnp.zeros((k, width), F32)], axis=0)
        grams.append(dot(stack[: 3 * k], stack, NT, HIGHEST))
    half = blocks // 2
    pairs = [grams[i] + grams[i + half] for i in range(half)]
    out[...] = functools.reduce(lambda a, b: a + b, pairs)


def tail_kernel(gram_ref, s_ref, y_ref, z_ref, next_ref, coef_ref, fact_ref, upper, inverse):
    n, lanes = gram_ref.shape
    k, w = n // 3, 8
    shape = (w, lanes)
    lane = lax.broadcasted_iota(jnp.int32, shape, 1)
    held = [gram_ref[i * w : (i + 1) * w, :] for i in range(n // w)]

    def spread(x):
        return jnp.broadcast_to(x, shape)

    for j in range(n // w):
        at = j * w
        inside = (lane >= at) & (lane < at + w)
        columns = [spread(held[j][:, at + c : at + c + 1]) for c in range(w)]
        p = [[spread(columns[b][a : a + 1, :]) if a <= b else None for b in range(w)] for a in range(w)]
        rows = [
            jnp.where(inside, jnp.where(lane == at + a, 1.0, 0.0), spread(held[j][a : a + 1, :]))
            for a in range(w)
        ]
        inv, m = [], [[None] * w for _ in range(w)]
        for c in range(w):
            inv.append(1.0 / p[c][c])
            for a in range(c + 1, w):
                m[a][c] = p[c][a] * inv[c]
                for b in range(a, w):
                    p[a][b] = p[a][b] - m[a][c] * p[c][b]
                rows[a] = rows[a] - m[a][c] * rows[c]
        for i in range(j + 1, n // w):
            f = []
            for c in range(w):
                value = spread(held[i][:, at + c : at + c + 1])
                for d in range(c):
                    value = value - f[d] * m[c][d]
                f.append(value)
            new = jnp.where(inside, 0.0, held[i])
            for c in range(w):
                new = new - (f[c] * inv[c]) * rows[c]
            held[i] = new
        for a in range(w):
            root = lax.rsqrt(p[a][a])
            row = rows[a] * root
            diag = jnp.zeros(shape, F32)
            for b in range(a, w):
                diag = jnp.where(lane == at + b, p[a][b], diag)
            inverse[at + a : at + a + 1, :] = jnp.where(lane < at + w, row, 0.0)[:1]
            upper[at + a : at + a + 1, :] = jnp.where(lane >= at + w, row, diag * root)[:1]
    x, u = inverse[...], upper[...]
    u12, u13 = u[:k, k : 2 * k], u[:k, 2 * k : 3 * k]
    u22, u23 = u[k : 2 * k, k : 2 * k], u[k : 2 * k, 2 * k : 3 * k]
    u33 = u[2 * k : 3 * k, 2 * k : 3 * k]
    x11, x22 = x[:k, :k], x[k : 2 * k, k : 2 * k]
    fact_ref[0] = dot(x11, u22, NT, HIGHEST)
    fact_ref[1] = dot(x22, u33, NT, HIGHEST)
    coef_ref[0, :, :k] = dot(x11, u12, NT, HIGHEST)
    coef_ref[0, :, k:] = jnp.zeros((k, k), F32)
    v = dot(x11, u12, TN, HIGHEST)
    coef_ref[1, :, :k] = dot(x22, u23 - dot(u22, v, NN, HIGHEST), NT, HIGHEST)
    coef_ref[1, :, k:] = dot(x22, u13 - dot(u12, v, NN, HIGHEST), NT, HIGHEST)
    stack = jnp.concatenate([s_ref[0], y_ref[0], z_ref[0]], axis=0)
    next_ref[...] = dot(x[2 * k : 3 * k, : 3 * k], stack, NN, HIGHEST)


def moved(x, axis, target):
    size = lax.axis_size(axis)
    return lax.ppermute(x, axis, [(i, target(i) % size) for i in range(size)])


def shifted(x, axis, by):
    return moved(x, axis, lambda i: i + by)


def sum_of_ring(x, ring):
    first, second, third = ring(1), ring(2), ring(3)
    return (x + second) + (first + third)


def body(tiles, tile_row, tile_col, tile_round, tile_count, start_block):
    tiles = tiles[0, 0]
    slots, edge = tiles.shape[0], tiles.shape[1]
    k = start_block.shape[0]
    members = lax.axis_size("rep")
    devices = lax.axis_size("rows")
    blocks = members
    offsets = [max(1, devices // 2**r) for r in range(1, ROUNDS + 1)]
    held_shape = (blocks, k, edge)
    smem = pl.BlockSpec(memory_space=pltpu.SMEM)
    vmem = pl.BlockSpec(memory_space=pltpu.VMEM)
    hbm = pl.BlockSpec(memory_space=pltpu.HBM)
    block_shape = jax.ShapeDtypeStruct(held_shape, F32)
    params = pltpu.CompilerParams(vmem_limit_bytes=VMEM_LIMIT)
    cost = pl.CostEstimate(
        flops=4 * slots * edge * edge * k, bytes_accessed=2 * slots * edge * edge, transcendentals=0
    )

    def scratch(sources, targets):
        return [pltpu.VMEM((sources, 2 * k, edge), BF16), pltpu.VMEM((targets + 1, k, edge), F32)]

    held, meta = pl.pallas_call(
        stage_kernel,
        out_shape=[jax.ShapeDtypeStruct(tiles.shape, BF16), jax.ShapeDtypeStruct((3, slots), jnp.int32)],
        in_specs=[hbm] * 5,
        out_specs=[vmem, smem],
        scratch_shapes=[pltpu.SMEM((1, 1, slots), jnp.int32)] * 3
        + [pltpu.SMEM((1, 1), jnp.int32), pltpu.SemaphoreType.DMA((5,))],
        compiler_params=params,
        cost_estimate=pl.CostEstimate(flops=0, bytes_accessed=2 * slots * edge * edge, transcendentals=0),
    )(tile_row, tile_col, tile_round, tile_count, tiles)

    backward = pl.pallas_call(
        backward_kernel,
        out_shape=[block_shape] * (ROUNDS + 1),
        in_specs=[smem, vmem, vmem],
        out_specs=[vmem] * (ROUNDS + 1),
        scratch_shapes=scratch(blocks, (ROUNDS + 1) * blocks),
        compiler_params=params,
        cost_estimate=cost,
    )
    forward = pl.pallas_call(
        forward_kernel,
        out_shape=block_shape,
        in_specs=[smem] + [vmem] * (ROUNDS + 3),
        out_specs=vmem,
        scratch_shapes=scratch((ROUNDS + 1) * blocks, blocks),
        compiler_params=params,
        cost_estimate=cost,
    )

    def rep_sum(part):
        return sum_of_ring(part, lambda by: jnp.roll(shifted(part, "rep", by), by, axis=0))

    def apply(q):
        _, quarter, _, last = offsets
        kept, out32, out16, out8, out4 = backward(meta, held, q)
        got4 = shifted(q, "rows", -last)
        got16 = shifted(q, "rows", -quarter)
        u = shifted(out8, "rows", last)
        w = shifted(out32, "rows", quarter)
        got8 = shifted(got4, "rows", -last)
        got32 = shifted(got16, "rows", -quarter)
        v = shifted(out4 + u, "rows", last)
        x = shifted(out16 + w, "rows", quarter)
        part = forward(meta, held, kept, q, got32, got16, got8, got4)
        return rep_sum(part + v + x)

    start = jnp.stack([start_block] + [shifted(start_block, "rep", by) for by in range(1, members)], 0)
    first = apply(start)
    second = apply(first)
    gram = pl.pallas_call(
        gram_kernel,
        out_shape=jax.ShapeDtypeStruct((3 * k, 4 * k), F32),
        in_specs=[vmem] * 3,
        out_specs=vmem,
        compiler_params=params,
    )(start, first, second)
    gram = gram + moved(gram, "rows", lambda i: i ^ 1)
    gram = sum_of_ring(gram, lambda by: shifted(gram, "rows", by * (devices // 4)))
    gram = gram + moved(gram, "rows", lambda i: i ^ 8)
    gram = sum_of_ring(gram, lambda by: moved(gram, "rows", lambda i: (i & ~7) | ((i + 2 * by) & 7)))
    result, coefficients, factors = pl.pallas_call(
        tail_kernel,
        out_shape=[
            jax.ShapeDtypeStruct((k, edge), F32),
            jax.ShapeDtypeStruct((2, k, 2 * k), F32),
            jax.ShapeDtypeStruct((2, k, k), F32),
        ],
        in_specs=[vmem] * 4,
        out_specs=[vmem] * 3,
        scratch_shapes=[pltpu.VMEM((3 * k, 4 * k), F32), pltpu.VMEM((3 * k, 4 * k), F32)],
        compiler_params=params,
    )(gram, start, first, second)
    return result, jnp.swapaxes(coefficients, 1, 2), factors


def solution(mesh):
    placed = (
        P("rows", "rep", None, None, None),
        P("rows", "rep", None),
        P("rows", "rep", None),
        P("rows", "rep", None),
        P("rows", "rep"),
        P(None, ("rows", "rep")),
    )
    return jax.shard_map(
        body,
        mesh=mesh,
        in_specs=placed,
        out_specs=(P(None, ("rows", "rep")), P(), P()),
        check_vma=False,
    )
```

```python
import functools

import jax
import jax.numpy as jnp
from jax import lax
from jax.experimental import pallas as pl
from jax.experimental.pallas import tpu as pltpu
from jax.sharding import PartitionSpec as P

ROUNDS = 4
F32 = jnp.float32
BF16 = jnp.bfloat16
HIGHEST = lax.Precision.HIGHEST
VMEM_LIMIT = 40 * 1024 * 1024


def dot(a, b, dims, precision=None):
    return lax.dot_general(a, b, (dims, ((), ())), precision=precision, preferred_element_type=F32)


NN = ((1,), (0,))
NT = ((1,), (1,))
TN = ((0,), (0,))


def split(x):
    high = x.astype(BF16)
    low = (x - high.astype(F32)).astype(BF16)
    return jnp.concatenate([high, low], axis=0)


def backward_kernel(meta, held, q_ref, *rest):
    outs, (terms, total) = rest[:-2], rest[-2:]
    blocks = q_ref.shape[0]
    trash = total.shape[0] - 1
    for b in range(blocks):
        terms[b] = split(q_ref[b])
    total[...] = jnp.zeros_like(total)
    for t in range(held.shape[0]):
        source = meta[1, t]
        target = jnp.where(meta[2, t] > 0, meta[0, t], trash)
        product = dot(terms[source], held[t], NN)
        half = product.shape[0] // 2
        total[target] += product[:half] + product[half:]
    for i, out in enumerate(outs):
        out[...] = total[i * blocks : (i + 1) * blocks]


def forward_kernel(meta, held, kept_ref, *rest):
    sources, out, (terms, total) = rest[: ROUNDS + 1], rest[ROUNDS + 1], rest[-2:]
    blocks = kept_ref.shape[0]
    trash = blocks
    for i, ref in enumerate(sources):
        for b in range(blocks):
            terms[i * blocks + b] = split(ref[b])
    total[:blocks] = kept_ref[...]
    total[trash] = jnp.zeros(total.shape[1:], F32)
    for t in range(held.shape[0]):
        source = meta[0, t]
        target = jnp.where(meta[2, t] > 0, meta[1, t], trash)
        product = dot(terms[source], held[t], NT)
        half = product.shape[0] // 2
        total[target] += product[:half] + product[half:]
    out[...] = total[:blocks]


def gram_kernel(s_ref, y_ref, z_ref, out):
    blocks, k, width = s_ref.shape
    grams = []
    for b in range(blocks):
        stack = jnp.concatenate([s_ref[b], y_ref[b], z_ref[b], jnp.zeros((k, width), F32)], axis=0)
        grams.append(dot(stack[: 3 * k], stack, NT, HIGHEST))
    half = blocks // 2
    pairs = [grams[i] + grams[i + half] for i in range(half)]
    gram = functools.reduce(lambda a, b: a + b, pairs)
    out[:k] = jnp.concatenate([gram[:k, : 3 * k], gram[2 * k :, 2 * k : 3 * k]], axis=1)
    rows = k // 2
    cut = [gram[k + i * rows : k + (i + 1) * rows, k : 3 * k] for i in range(2)]
    out[k:] = jnp.concatenate(cut, axis=1)


def tail_kernel(gram_ref, s_ref, y_ref, z_ref, next_ref, coef_ref, fact_ref, upper, inverse):
    lanes, w = gram_ref.shape[1], 8
    k = lanes // 4
    n = 3 * k
    shape = (w, lanes)
    lane = lax.broadcasted_iota(jnp.int32, shape, 1)
    main, below = gram_ref[:k, :], gram_ref[k:, :]
    sy, sz, zz = main[:, k : 2 * k], main[:, 2 * k : 3 * k], main[:, 3 * k :]
    cut = jnp.concatenate([below[:, : 2 * k], below[:, 2 * k :]], axis=0)
    yz = cut[:, k:]
    zero = jnp.zeros((k, k), F32)
    upper[:k] = main
    upper[k : 2 * k] = jnp.concatenate([sy.T, cut, zero], axis=1)
    upper[2 * k :] = jnp.concatenate([sz.T, yz.T, zz, zero], axis=1)
    held = [upper[i * w : (i + 1) * w, :] for i in range(n // w)]
    for i in range(k // w):
        held[i] = jnp.where(lane < n, held[i], 0.0)

    def spread(x):
        return jnp.broadcast_to(x, shape)

    for j in range(n // w):
        at = j * w
        inside = (lane >= at) & (lane < at + w)
        columns = [spread(held[j][:, at + c : at + c + 1]) for c in range(w)]
        p = [[spread(columns[b][a : a + 1, :]) if a <= b else None for b in range(w)] for a in range(w)]
        rows = [
            jnp.where(inside, jnp.where(lane == at + a, 1.0, 0.0), spread(held[j][a : a + 1, :]))
            for a in range(w)
        ]
        inv, m = [], [[None] * w for _ in range(w)]
        for c in range(w):
            inv.append(1.0 / p[c][c])
            for a in range(c + 1, w):
                m[a][c] = p[c][a] * inv[c]
                for b in range(a, w):
                    p[a][b] = p[a][b] - m[a][c] * p[c][b]
                rows[a] = rows[a] - m[a][c] * rows[c]
        for i in range(j + 1, n // w):
            f = []
            for c in range(w):
                value = spread(held[i][:, at + c : at + c + 1])
                for d in range(c):
                    value = value - f[d] * m[c][d]
                f.append(value)
            new = jnp.where(inside, 0.0, held[i])
            for c in range(w):
                new = new - (f[c] * inv[c]) * rows[c]
            held[i] = new
        for a in range(w):
            root = lax.rsqrt(p[a][a])
            row = rows[a] * root
            diag = jnp.zeros(shape, F32)
            for b in range(a, w):
                diag = jnp.where(lane == at + b, p[a][b], diag)
            inverse[at + a : at + a + 1, :] = jnp.where(lane < at + w, row, 0.0)[:1]
            upper[at + a : at + a + 1, :] = jnp.where(lane >= at + w, row, diag * root)[:1]
    x, u = inverse[...], upper[...]
    u12, u13 = u[:k, k : 2 * k], u[:k, 2 * k : 3 * k]
    u22, u23 = u[k : 2 * k, k : 2 * k], u[k : 2 * k, 2 * k : 3 * k]
    u33 = u[2 * k : 3 * k, 2 * k : 3 * k]
    x11, x22 = x[:k, :k], x[k : 2 * k, k : 2 * k]
    fact_ref[0] = dot(x11, u22, NT, HIGHEST)
    fact_ref[1] = dot(x22, u33, NT, HIGHEST)
    coef_ref[0, :, :k] = dot(x11, u12, NT, HIGHEST)
    coef_ref[0, :, k:] = jnp.zeros((k, k), F32)
    v = dot(x11, u12, TN, HIGHEST)
    coef_ref[1, :, :k] = dot(x22, u23 - dot(u22, v, NN, HIGHEST), NT, HIGHEST)
    coef_ref[1, :, k:] = dot(x22, u13 - dot(u12, v, NN, HIGHEST), NT, HIGHEST)
    stack = jnp.concatenate([s_ref[0], y_ref[0], z_ref[0]], axis=0)
    next_ref[...] = dot(x[2 * k : 3 * k, : 3 * k], stack, NN, HIGHEST)


def moved(x, axis, target):
    size = lax.axis_size(axis)
    return lax.ppermute(x, axis, [(i, target(i) % size) for i in range(size)])


def shifted(x, axis, by):
    return moved(x, axis, lambda i: i + by)


def sum_of_ring(x, ring):
    first, second, third = ring(1), ring(2), ring(3)
    return (x + second) + (first + third)


def body(tiles, tile_row, tile_col, tile_round, tile_count, start_block):
    tiles = tiles[0, 0]
    slots, edge = tiles.shape[0], tiles.shape[1]
    k = start_block.shape[0]
    members = lax.axis_size("rep")
    devices = lax.axis_size("rows")
    blocks = members
    offsets = [max(1, devices // 2**r) for r in range(1, ROUNDS + 1)]
    held_shape = (blocks, k, edge)
    smem = pl.BlockSpec(memory_space=pltpu.SMEM)
    vmem = pl.BlockSpec(memory_space=pltpu.VMEM)
    block_shape = jax.ShapeDtypeStruct(held_shape, F32)
    params = pltpu.CompilerParams(vmem_limit_bytes=VMEM_LIMIT)
    cost = pl.CostEstimate(
        flops=4 * slots * edge * edge * k, bytes_accessed=2 * slots * edge * edge, transcendentals=0
    )

    def scratch(sources, targets):
        return [pltpu.VMEM((sources, 2 * k, edge), BF16), pltpu.VMEM((targets + 1, k, edge), F32)]

    member = lax.axis_index("rep")
    column = lax.rem(member - tile_col[0, 0] + blocks, blocks)
    row = lax.rem(member - tile_row[0, 0] + blocks, blocks)
    live = (jnp.arange(slots, dtype=jnp.int32) < tile_count[0]).astype(jnp.int32)
    meta = jnp.stack([tile_round[0, 0] * blocks + column, row, live], 0)
    backward = pl.pallas_call(
        backward_kernel,
        out_shape=[block_shape] * (ROUNDS + 1),
        in_specs=[smem, vmem, vmem],
        out_specs=[vmem] * (ROUNDS + 1),
        scratch_shapes=scratch(blocks, (ROUNDS + 1) * blocks),
        compiler_params=params,
        cost_estimate=cost,
    )
    forward = pl.pallas_call(
        forward_kernel,
        out_shape=block_shape,
        in_specs=[smem] + [vmem] * (ROUNDS + 3),
        out_specs=vmem,
        scratch_shapes=scratch((ROUNDS + 1) * blocks, blocks),
        compiler_params=params,
        cost_estimate=cost,
    )

    def rep_sum(part):
        return sum_of_ring(part, lambda by: jnp.roll(shifted(part, "rep", by), by, axis=0))

    def apply(q):
        _, quarter, _, last = offsets
        kept, out32, out16, out8, out4 = backward(meta, tiles, q)
        got4 = shifted(q, "rows", -last)
        got16 = shifted(q, "rows", -quarter)
        u = shifted(out8, "rows", last)
        w = shifted(out32, "rows", quarter)
        got8 = shifted(got4, "rows", -last)
        got32 = shifted(got16, "rows", -quarter)
        v = shifted(out4 + u, "rows", last)
        x = shifted(out16 + w, "rows", quarter)
        part = forward(meta, tiles, kept, q, got32, got16, got8, got4)
        return rep_sum(part + v + x)

    start = jnp.stack([start_block] + [shifted(start_block, "rep", by) for by in range(1, members)], 0)
    first = apply(start)
    second = apply(first)
    gram = pl.pallas_call(
        gram_kernel,
        out_shape=jax.ShapeDtypeStruct((k + k // 2, 4 * k), F32),
        in_specs=[vmem] * 3,
        out_specs=vmem,
        compiler_params=params,
    )(start, first, second)
    gram = gram + moved(gram, "rows", lambda i: i ^ 1)
    gram = sum_of_ring(gram, lambda by: shifted(gram, "rows", by * (devices // 4)))
    def along_z(by):
        return moved(gram, "rows", lambda i: (i & ~14) | ((i + (2 * by if i & 1 else -2 * by)) & 14))

    near, middle, far, opposite = along_z(1), along_z(2), along_z(3), along_z(4)
    near2, middle2, far2 = [moved(x, "rows", lambda i: i ^ 1) for x in (near, middle, far)]
    gram = ((gram + opposite) + (middle + middle2)) + ((near + far2) + (far + near2))
    result, coefficients, factors = pl.pallas_call(
        tail_kernel,
        out_shape=[
            jax.ShapeDtypeStruct((k, edge), F32),
            jax.ShapeDtypeStruct((2, k, 2 * k), F32),
            jax.ShapeDtypeStruct((2, k, k), F32),
        ],
        in_specs=[vmem] * 4,
        out_specs=[vmem] * 3,
        scratch_shapes=[pltpu.VMEM((3 * k, 4 * k), F32), pltpu.VMEM((3 * k, 4 * k), F32)],
        compiler_params=params,
    )(gram, start, first, second)
    return result, jnp.swapaxes(coefficients, 1, 2), factors


def solution(mesh):
    placed = (
        P("rows", "rep", None, None, None),
        P("rows", "rep", None),
        P("rows", "rep", None),
        P("rows", "rep", None),
        P("rows", "rep"),
        P(None, ("rows", "rep")),
    )
    return jax.shard_map(
        body,
        mesh=mesh,
        in_specs=placed,
        out_specs=(P(None, ("rows", "rep")), P(), P()),
        check_vma=False,
    )
```

```python
import functools

import jax
import jax.numpy as jnp
from jax import lax
from jax.experimental import pallas as pl
from jax.experimental.pallas import tpu as pltpu
from jax.sharding import PartitionSpec as P

ROUNDS = 4
F32 = jnp.float32
BF16 = jnp.bfloat16
HIGHEST = lax.Precision.HIGHEST
VMEM_LIMIT = 40 * 1024 * 1024


def dot(a, b, dims, precision=None):
    return lax.dot_general(a, b, (dims, ((), ())), precision=precision, preferred_element_type=F32)


NN = ((1,), (0,))
NT = ((1,), (1,))
TN = ((0,), (0,))


def split(x):
    high = x.astype(BF16)
    low = (x - high.astype(F32)).astype(BF16)
    return jnp.concatenate([high, low], axis=0)


def ready_kernel(tiles_ref, start_ref, start_out):
    start_out[...] = start_ref[...]


def backward_kernel(meta, held, q_ref, *rest):
    outs, (terms, total) = rest[:-2], rest[-2:]
    blocks = q_ref.shape[0]
    trash = total.shape[0] - 1
    for b in range(blocks):
        terms[b] = split(q_ref[b])
    total[...] = jnp.zeros_like(total)
    for t in range(held.shape[0]):
        source = meta[1, t]
        target = jnp.where(meta[2, t] > 0, meta[0, t], trash)
        product = dot(terms[source], held[t], NN)
        half = product.shape[0] // 2
        total[target] += product[:half] + product[half:]
    for i, out in enumerate(outs):
        out[...] = total[i * blocks : (i + 1) * blocks]


def forward_kernel(meta, held, kept_ref, *rest):
    sources, out, (terms, total) = rest[: ROUNDS + 1], rest[ROUNDS + 1], rest[-2:]
    blocks = kept_ref.shape[0]
    trash = blocks
    for i, ref in enumerate(sources):
        for b in range(blocks):
            terms[i * blocks + b] = split(ref[b])
    total[:blocks] = kept_ref[...]
    total[trash] = jnp.zeros(total.shape[1:], F32)
    for t in range(held.shape[0]):
        source = meta[0, t]
        target = jnp.where(meta[2, t] > 0, meta[1, t], trash)
        product = dot(terms[source], held[t], NT)
        half = product.shape[0] // 2
        total[target] += product[:half] + product[half:]
    out[...] = total[:blocks]


def gram_kernel(s_ref, y_ref, z_ref, out):
    blocks, k, width = s_ref.shape
    grams = []
    for b in range(blocks):
        stack = jnp.concatenate([s_ref[b], y_ref[b], z_ref[b], jnp.zeros((k, width), F32)], axis=0)
        grams.append(dot(stack[: 3 * k], stack, NT, HIGHEST))
    half = blocks // 2
    pairs = [grams[i] + grams[i + half] for i in range(half)]
    gram = functools.reduce(lambda a, b: a + b, pairs)
    out[:k] = jnp.concatenate([gram[:k, : 3 * k], gram[2 * k :, 2 * k : 3 * k]], axis=1)
    rows = k // 2
    cut = [gram[k + i * rows : k + (i + 1) * rows, k : 3 * k] for i in range(2)]
    out[k:] = jnp.concatenate(cut, axis=1)


def tail_kernel(gram_ref, s_ref, y_ref, z_ref, next_ref, coef_ref, fact_ref, upper, inverse):
    lanes, w = gram_ref.shape[1], 8
    k = lanes // 4
    n = 3 * k
    shape = (w, lanes)
    lane = lax.broadcasted_iota(jnp.int32, shape, 1)
    main, below = gram_ref[:k, :], gram_ref[k:, :]
    sy, sz, zz = main[:, k : 2 * k], main[:, 2 * k : 3 * k], main[:, 3 * k :]
    cut = jnp.concatenate([below[:, : 2 * k], below[:, 2 * k :]], axis=0)
    yz = cut[:, k:]
    zero = jnp.zeros((k, k), F32)
    upper[:k] = main
    upper[k : 2 * k] = jnp.concatenate([sy.T, cut, zero], axis=1)
    upper[2 * k :] = jnp.concatenate([sz.T, yz.T, zz, zero], axis=1)
    held = [upper[i * w : (i + 1) * w, :] for i in range(n // w)]
    for i in range(k // w):
        held[i] = jnp.where(lane < n, held[i], 0.0)

    def spread(x):
        return jnp.broadcast_to(x, shape)

    for j in range(n // w):
        at = j * w
        if at == 2 * k:
            x11, x22 = inverse[:k, :k], inverse[k : 2 * k, k : 2 * k]
            u12, u13 = upper[:k, k : 2 * k], upper[:k, 2 * k : n]
            u22, u23 = upper[k : 2 * k, k : 2 * k], upper[k : 2 * k, 2 * k : n]
            fact_ref[0] = dot(x11, u22, NT, HIGHEST)
            coef_ref[0, :, :k] = dot(x11, u12, NT, HIGHEST)
            coef_ref[0, :, k:] = jnp.zeros((k, k), F32)
            v = dot(x11, u12, TN, HIGHEST)
            coef_ref[1, :, :k] = dot(x22, u23 - dot(u22, v, NN, HIGHEST), NT, HIGHEST)
            coef_ref[1, :, k:] = dot(x22, u13 - dot(u12, v, NN, HIGHEST), NT, HIGHEST)
        inside = (lane >= at) & (lane < at + w)
        columns = [spread(held[j][:, at + c : at + c + 1]) for c in range(w)]
        p = [[spread(columns[b][a : a + 1, :]) if a <= b else None for b in range(w)] for a in range(w)]
        rows = [
            jnp.where(inside, jnp.where(lane == at + a, 1.0, 0.0), spread(held[j][a : a + 1, :]))
            for a in range(w)
        ]
        inv, m = [], [[None] * w for _ in range(w)]
        for c in range(w):
            inv.append(1.0 / p[c][c])
            for a in range(c + 1, w):
                m[a][c] = p[c][a] * inv[c]
                for b in range(a, w):
                    p[a][b] = p[a][b] - m[a][c] * p[c][b]
                rows[a] = rows[a] - m[a][c] * rows[c]
        for i in range(j + 1, n // w):
            f = []
            for c in range(w):
                value = spread(held[i][:, at + c : at + c + 1])
                for d in range(c):
                    value = value - f[d] * m[c][d]
                f.append(value)
            new = jnp.where(inside, 0.0, held[i])
            for c in range(w):
                new = new - (f[c] * inv[c]) * rows[c]
            held[i] = new
        for a in range(w):
            root = lax.rsqrt(p[a][a])
            row = rows[a] * root
            diag = jnp.zeros(shape, F32)
            for b in range(a, w):
                diag = jnp.where(lane == at + b, p[a][b], diag)
            inverse[at + a : at + a + 1, :] = jnp.where(lane < at + w, row, 0.0)[:1]
            upper[at + a : at + a + 1, :] = jnp.where(lane >= at + w, row, diag * root)[:1]
    fact_ref[1] = dot(x22, upper[2 * k :, 2 * k : n], NT, HIGHEST)
    stack = jnp.concatenate([s_ref[0], y_ref[0], z_ref[0]], axis=0)
    next_ref[...] = dot(inverse[2 * k :, :n], stack, NN, HIGHEST)


def moved(x, axis, target):
    size = lax.axis_size(axis)
    return lax.ppermute(x, axis, [(i, target(i) % size) for i in range(size)])


def shifted(x, axis, by):
    return moved(x, axis, lambda i: i + by)


def sum_of_ring(x, ring):
    first, second, third = ring(1), ring(2), ring(3)
    return (x + second) + (first + third)


def body(tiles, tile_row, tile_col, tile_round, tile_count, start_block):
    tiles = tiles[0, 0]
    slots, edge = tiles.shape[0], tiles.shape[1]
    k = start_block.shape[0]
    members = lax.axis_size("rep")
    devices = lax.axis_size("rows")
    blocks = members
    offsets = [max(1, devices // 2**r) for r in range(1, ROUNDS + 1)]
    held_shape = (blocks, k, edge)
    smem = pl.BlockSpec(memory_space=pltpu.SMEM)
    vmem = pl.BlockSpec(memory_space=pltpu.VMEM)
    block_shape = jax.ShapeDtypeStruct(held_shape, F32)
    params = pltpu.CompilerParams(vmem_limit_bytes=VMEM_LIMIT)
    cost = pl.CostEstimate(
        flops=4 * slots * edge * edge * k, bytes_accessed=2 * slots * edge * edge, transcendentals=0
    )

    def scratch(sources, targets):
        return [pltpu.VMEM((sources, 2 * k, edge), BF16), pltpu.VMEM((targets + 1, k, edge), F32)]

    member = lax.axis_index("rep")
    column = lax.rem(member - tile_col[0, 0] + blocks, blocks)
    row = lax.rem(member - tile_row[0, 0] + blocks, blocks)
    live = (jnp.arange(slots, dtype=jnp.int32) < tile_count[0]).astype(jnp.int32)
    meta = jnp.stack([tile_round[0, 0] * blocks + column, row, live], 0)
    own = pl.pallas_call(
        ready_kernel,
        out_shape=jax.ShapeDtypeStruct(start_block.shape, F32),
        in_specs=[vmem, vmem],
        out_specs=vmem,
        compiler_params=params,
    )(tiles, start_block)
    backward = pl.pallas_call(
        backward_kernel,
        out_shape=[block_shape] * (ROUNDS + 1),
        in_specs=[smem, vmem, vmem],
        out_specs=[vmem] * (ROUNDS + 1),
        scratch_shapes=scratch(blocks, (ROUNDS + 1) * blocks),
        compiler_params=params,
        cost_estimate=cost,
    )
    forward = pl.pallas_call(
        forward_kernel,
        out_shape=block_shape,
        in_specs=[smem] + [vmem] * (ROUNDS + 3),
        out_specs=vmem,
        scratch_shapes=scratch((ROUNDS + 1) * blocks, blocks),
        compiler_params=params,
        cost_estimate=cost,
    )

    def rep_sum(part):
        return sum_of_ring(part, lambda by: jnp.roll(shifted(part, "rep", by), by, axis=0))

    def apply(q):
        _, quarter, _, last = offsets
        kept, out32, out16, out8, out4 = backward(meta, tiles, q)
        got4 = shifted(q, "rows", -last)
        got16 = shifted(q, "rows", -quarter)
        u = shifted(out8, "rows", last)
        w = shifted(out32, "rows", quarter)
        got8 = shifted(got4, "rows", -last)
        got32 = shifted(got16, "rows", -quarter)
        v = shifted(out4 + u, "rows", last)
        x = shifted(out16 + w, "rows", quarter)
        part = forward(meta, tiles, kept, q, got32, got16, got8, got4)
        return rep_sum(part + v + x)

    start = jnp.stack([own] + [shifted(start_block, "rep", by) for by in range(1, members)], 0)
    first = apply(start)
    second = apply(first)
    gram = pl.pallas_call(
        gram_kernel,
        out_shape=jax.ShapeDtypeStruct((k + k // 2, 4 * k), F32),
        in_specs=[vmem] * 3,
        out_specs=vmem,
        compiler_params=params,
    )(start, first, second)
    gram = gram + moved(gram, "rows", lambda i: i ^ 1)
    gram = sum_of_ring(gram, lambda by: shifted(gram, "rows", by * (devices // 4)))
    def along_z(by):
        return moved(gram, "rows", lambda i: (i & ~14) | ((i + (2 * by if i & 1 else -2 * by)) & 14))

    near, middle, far, opposite = along_z(1), along_z(2), along_z(3), along_z(4)
    near2, middle2, far2 = [moved(x, "rows", lambda i: i ^ 1) for x in (near, middle, far)]
    gram = ((gram + opposite) + (middle + middle2)) + ((near + far2) + (far + near2))
    result, coefficients, factors = pl.pallas_call(
        tail_kernel,
        out_shape=[
            jax.ShapeDtypeStruct((k, edge), F32),
            jax.ShapeDtypeStruct((2, k, 2 * k), F32),
            jax.ShapeDtypeStruct((2, k, k), F32),
        ],
        in_specs=[vmem] * 4,
        out_specs=[vmem] * 3,
        scratch_shapes=[pltpu.VMEM((3 * k, 4 * k), F32), pltpu.VMEM((3 * k, 4 * k), F32)],
        compiler_params=params,
    )(gram, start, first, second)
    return result, jnp.swapaxes(coefficients, 1, 2), factors


def solution(mesh):
    placed = (
        P("rows", "rep", None, None, None),
        P("rows", "rep", None),
        P("rows", "rep", None),
        P("rows", "rep", None),
        P("rows", "rep"),
        P(None, ("rows", "rep")),
    )
    return jax.shard_map(
        body,
        mesh=mesh,
        in_specs=placed,
        out_specs=(P(None, ("rows", "rep")), P(), P()),
        check_vma=False,
    )
```

```python
import functools

import jax
import jax.numpy as jnp
from jax import lax
from jax.experimental import pallas as pl
from jax.experimental.pallas import tpu as pltpu
from jax.sharding import PartitionSpec as P

ROUNDS = 4
F32 = jnp.float32
BF16 = jnp.bfloat16
HIGHEST = lax.Precision.HIGHEST
VMEM_LIMIT = 40 * 1024 * 1024


def dot(a, b, dims, precision=None):
    return lax.dot_general(a, b, (dims, ((), ())), precision=precision, preferred_element_type=F32)


NN = ((1,), (0,))
NT = ((1,), (1,))
TN = ((0,), (0,))


def split(x):
    high = x.astype(BF16)
    low = (x - high.astype(F32)).astype(BF16)
    return jnp.concatenate([high, low], axis=0)


def ready_kernel(tiles_ref, start_ref, start_out):
    start_out[...] = start_ref[...]


def backward_kernel(meta, held, q_ref, *rest):
    outs, (terms, total) = rest[:-2], rest[-2:]
    blocks = q_ref.shape[0]
    trash = total.shape[0] - 1
    for b in range(blocks):
        terms[b] = split(q_ref[b])
    total[...] = jnp.zeros_like(total)
    for t in range(held.shape[0]):
        source = meta[1, t]
        target = jnp.where(meta[2, t] > 0, meta[0, t], trash)
        product = dot(terms[source], held[t], NN)
        half = product.shape[0] // 2
        total[target] += product[:half] + product[half:]
    for i, out in enumerate(outs):
        out[...] = total[i * blocks : (i + 1) * blocks]


def forward_kernel(meta, held, kept_ref, *rest):
    sources, out, (terms, total) = rest[ROUNDS::-1], rest[ROUNDS + 1], rest[-2:]
    blocks = kept_ref.shape[0]
    trash = blocks
    for i, ref in enumerate(sources):
        for b in range(blocks):
            terms[i * blocks + b] = split(ref[b])
    total[:blocks] = kept_ref[...]
    total[trash] = jnp.zeros(total.shape[1:], F32)
    for t in range(held.shape[0]):
        source = meta[0, t]
        target = jnp.where(meta[2, t] > 0, meta[1, t], trash)
        product = dot(terms[source], held[t], NT)
        half = product.shape[0] // 2
        total[target] += product[:half] + product[half:]
    out[...] = total[:blocks]


def rep_sum_kernel(second, first, third, own, out):
    n = own.shape[0]
    for b in range(n):
        out[b] = (own[b] + second[(b - 2) % n]) + (first[(b - 1) % n] + third[(b - 3) % n])


def gram_kernel(s_ref, y_ref, z_ref, out):
    blocks, k, width = s_ref.shape
    grams = []
    for b in range(blocks):
        stack = jnp.concatenate([s_ref[b], y_ref[b], z_ref[b], jnp.zeros((k, width), F32)], axis=0)
        grams.append(dot(stack[: 3 * k], stack, NT, HIGHEST))
    half = blocks // 2
    pairs = [grams[i] + grams[i + half] for i in range(half)]
    gram = functools.reduce(lambda a, b: a + b, pairs)
    out[:k] = jnp.concatenate([gram[:k, : 3 * k], gram[2 * k :, 2 * k : 3 * k]], axis=1)
    rows = k // 2
    cut = [gram[k + i * rows : k + (i + 1) * rows, k : 3 * k] for i in range(2)]
    out[k:] = jnp.concatenate(cut, axis=1)


def tail_kernel(gram_ref, s_ref, y_ref, z_ref, next_ref, coef_ref, fact_ref, upper, inverse):
    lanes, w = gram_ref.shape[1], 8
    k = lanes // 4
    n = 3 * k
    shape = (w, lanes)
    lane = lax.broadcasted_iota(jnp.int32, shape, 1)
    main, below = gram_ref[:k, :], gram_ref[k:, :]
    sy, sz, zz = main[:, k : 2 * k], main[:, 2 * k : 3 * k], main[:, 3 * k :]
    cut = jnp.concatenate([below[:, : 2 * k], below[:, 2 * k :]], axis=0)
    yz = cut[:, k:]
    zero = jnp.zeros((k, k), F32)
    upper[:k] = main
    upper[k : 2 * k] = jnp.concatenate([sy.T, cut, zero], axis=1)
    upper[2 * k :] = jnp.concatenate([sz.T, yz.T, zz, zero], axis=1)
    held = [upper[i * w : (i + 1) * w, :] for i in range(n // w)]
    for i in range(k // w):
        held[i] = jnp.where(lane < n, held[i], 0.0)

    def spread(x):
        return jnp.broadcast_to(x, shape)

    for j in range(n // w):
        at = j * w
        if at == 2 * k:
            x11, x22 = inverse[:k, :k], inverse[k : 2 * k, k : 2 * k]
            u12, u13 = upper[:k, k : 2 * k], upper[:k, 2 * k : n]
            u22, u23 = upper[k : 2 * k, k : 2 * k], upper[k : 2 * k, 2 * k : n]
            fact_ref[0] = dot(x11, u22, NT, HIGHEST)
            coef_ref[0, :, :k] = dot(x11, u12, NT, HIGHEST)
            coef_ref[0, :, k:] = jnp.zeros((k, k), F32)
            v = dot(x11, u12, TN, HIGHEST)
            coef_ref[1, :, :k] = dot(x22, u23 - dot(u22, v, NN, HIGHEST), NT, HIGHEST)
            coef_ref[1, :, k:] = dot(x22, u13 - dot(u12, v, NN, HIGHEST), NT, HIGHEST)
        inside = (lane >= at) & (lane < at + w)
        columns = [spread(held[j][:, at + c : at + c + 1]) for c in range(w)]
        p = [[spread(columns[b][a : a + 1, :]) if a <= b else None for b in range(w)] for a in range(w)]
        rows = [
            jnp.where(inside, jnp.where(lane == at + a, 1.0, 0.0), spread(held[j][a : a + 1, :]))
            for a in range(w)
        ]
        inv, m = [], [[None] * w for _ in range(w)]
        for c in range(w):
            inv.append(1.0 / p[c][c])
            for a in range(c + 1, w):
                m[a][c] = p[c][a] * inv[c]
                for b in range(a, w):
                    p[a][b] = p[a][b] - m[a][c] * p[c][b]
                rows[a] = rows[a] - m[a][c] * rows[c]
        for i in range(j + 1, n // w):
            f = []
            for c in range(w):
                value = spread(held[i][:, at + c : at + c + 1])
                for d in range(c):
                    value = value - f[d] * m[c][d]
                f.append(value)
            new = jnp.where(inside, 0.0, held[i])
            for c in range(w):
                new = new - (f[c] * inv[c]) * rows[c]
            held[i] = new
        for a in range(w):
            root = lax.rsqrt(p[a][a])
            row = rows[a] * root
            diag = jnp.zeros(shape, F32)
            for b in range(a, w):
                diag = jnp.where(lane == at + b, p[a][b], diag)
            inverse[at + a : at + a + 1, :] = jnp.where(lane < at + w, row, 0.0)[:1]
            upper[at + a : at + a + 1, :] = jnp.where(lane >= at + w, row, diag * root)[:1]
    fact_ref[1] = dot(x22, upper[2 * k :, 2 * k : n], NT, HIGHEST)
    stack = jnp.concatenate([s_ref[0], y_ref[0], z_ref[0]], axis=0)
    next_ref[...] = dot(inverse[2 * k :, :n], stack, NN, HIGHEST)


def moved(x, axis, target):
    size = lax.axis_size(axis)
    return lax.ppermute(x, axis, [(i, target(i) % size) for i in range(size)])


def shifted(x, axis, by):
    return moved(x, axis, lambda i: i + by)


def sum_of_ring(x, ring):
    first, second, third = ring(1), ring(2), ring(3)
    return (x + second) + (first + third)


def body(tiles, tile_row, tile_col, tile_round, tile_count, start_block):
    tiles = tiles[0, 0]
    slots, edge = tiles.shape[0], tiles.shape[1]
    k = start_block.shape[0]
    members = lax.axis_size("rep")
    devices = lax.axis_size("rows")
    blocks = members
    offsets = [max(1, devices // 2**r) for r in range(1, ROUNDS + 1)]
    held_shape = (blocks, k, edge)
    smem = pl.BlockSpec(memory_space=pltpu.SMEM)
    vmem = pl.BlockSpec(memory_space=pltpu.VMEM)
    block_shape = jax.ShapeDtypeStruct(held_shape, F32)
    params = pltpu.CompilerParams(vmem_limit_bytes=VMEM_LIMIT)
    cost = pl.CostEstimate(
        flops=4 * slots * edge * edge * k, bytes_accessed=2 * slots * edge * edge, transcendentals=0
    )

    def scratch(sources, targets):
        return [pltpu.VMEM((sources, 2 * k, edge), BF16), pltpu.VMEM((targets + 1, k, edge), F32)]

    member = lax.axis_index("rep")
    column = lax.rem(member - tile_col[0, 0] + blocks, blocks)
    row = lax.rem(member - tile_row[0, 0] + blocks, blocks)
    live = (jnp.arange(slots, dtype=jnp.int32) < tile_count[0]).astype(jnp.int32)
    meta = jnp.stack([(tile_round[0, 0] * blocks + column) * live, row * live, live], 0)
    own = pl.pallas_call(
        ready_kernel,
        out_shape=jax.ShapeDtypeStruct(start_block.shape, F32),
        in_specs=[vmem, vmem],
        out_specs=vmem,
        compiler_params=params,
    )(tiles, start_block)
    backward = pl.pallas_call(
        backward_kernel,
        out_shape=[block_shape] * (ROUNDS + 1),
        in_specs=[smem, vmem, vmem],
        out_specs=[vmem] * (ROUNDS + 1),
        scratch_shapes=scratch(blocks, (ROUNDS + 1) * blocks),
        compiler_params=params,
        cost_estimate=cost,
    )
    forward = pl.pallas_call(
        forward_kernel,
        out_shape=block_shape,
        in_specs=[smem] + [vmem] * (ROUNDS + 3),
        out_specs=vmem,
        scratch_shapes=scratch((ROUNDS + 1) * blocks, blocks),
        compiler_params=params,
        cost_estimate=cost,
    )

    def rep_sum(part):
        return pl.pallas_call(
            rep_sum_kernel,
            out_shape=block_shape,
            in_specs=[vmem] * 4,
            out_specs=vmem,
            compiler_params=params,
        )(*[shifted(part, "rep", by) for by in (2, 1, 3)], part)

    def apply(q):
        _, quarter, _, last = offsets
        kept, out32, out16, out8, out4 = backward(meta, tiles, q)
        got4 = shifted(q, "rows", -last)
        got16 = shifted(q, "rows", -quarter)
        u = shifted(out8, "rows", last)
        w = shifted(out32, "rows", quarter)
        got8 = shifted(got4, "rows", -last)
        got32 = shifted(got16, "rows", -quarter)
        v = shifted(out4 + u, "rows", last)
        x = shifted(out16 + w, "rows", quarter)
        part = forward(meta, tiles, kept, got4, got8, got16, got32, q)
        return rep_sum(part + v + x)

    start = jnp.stack([own] + [shifted(start_block, "rep", by) for by in range(1, members)], 0)
    first = apply(start)
    second = apply(first)
    gram = pl.pallas_call(
        gram_kernel,
        out_shape=jax.ShapeDtypeStruct((k + k // 2, 4 * k), F32),
        in_specs=[vmem] * 3,
        out_specs=vmem,
        compiler_params=params,
    )(start, first, second)
    gram = gram + moved(gram, "rows", lambda i: i ^ 1)
    gram = sum_of_ring(gram, lambda by: shifted(gram, "rows", by * (devices // 4)))
    def along_z(by):
        return moved(gram, "rows", lambda i: (i & ~14) | ((i + (2 * by if i & 1 else -2 * by)) & 14))

    near, middle, far, opposite = along_z(1), along_z(2), along_z(3), along_z(4)
    near2, middle2, far2 = [moved(x, "rows", lambda i: i ^ 1) for x in (near, middle, far)]
    gram = ((gram + opposite) + (middle + middle2)) + ((near + far2) + (far + near2))
    result, coefficients, factors = pl.pallas_call(
        tail_kernel,
        out_shape=[
            jax.ShapeDtypeStruct((k, edge), F32),
            jax.ShapeDtypeStruct((2, k, 2 * k), F32),
            jax.ShapeDtypeStruct((2, k, k), F32),
        ],
        in_specs=[vmem] * 4,
        out_specs=[vmem] * 3,
        scratch_shapes=[pltpu.VMEM((3 * k, 4 * k), F32), pltpu.VMEM((3 * k, 4 * k), F32)],
        compiler_params=params,
    )(gram, start, first, second)
    return result, jnp.swapaxes(coefficients, 1, 2), factors


def solution(mesh):
    placed = (
        P("rows", "rep", None, None, None),
        P("rows", "rep", None),
        P("rows", "rep", None),
        P("rows", "rep", None),
        P("rows", "rep"),
        P(None, ("rows", "rep")),
    )
    return jax.shard_map(
        body,
        mesh=mesh,
        in_specs=placed,
        out_specs=(P(None, ("rows", "rep")), P(), P()),
        check_vma=False,
    )
```

```python
import functools

import jax
import jax.numpy as jnp
from jax import lax
from jax.experimental import pallas as pl
from jax.experimental.pallas import tpu as pltpu
from jax.sharding import PartitionSpec as P

ROUNDS = 4
F32 = jnp.float32
BF16 = jnp.bfloat16
HIGHEST = lax.Precision.HIGHEST
VMEM_LIMIT = 40 * 1024 * 1024


def dot(a, b, dims, precision=None):
    return lax.dot_general(a, b, (dims, ((), ())), precision=precision, preferred_element_type=F32)


NN = ((1,), (0,))
NT = ((1,), (1,))
TN = ((0,), (0,))


def split(x):
    high = x.astype(BF16)
    low = (x - high.astype(F32)).astype(BF16)
    return jnp.concatenate([high, low], axis=0)


def ready_kernel(tiles_ref, start_ref, start_out):
    start_out[...] = start_ref[...]


def backward_kernel(meta, held, q_ref, *rest):
    outs, (terms, total) = rest[:-2], rest[-2:]
    blocks = q_ref.shape[0]
    trash = total.shape[0] - 1
    for b in range(blocks):
        terms[b] = split(q_ref[b])
    total[...] = jnp.zeros_like(total)
    for t in range(held.shape[0]):
        source = meta[1, t]
        target = jnp.where(meta[2, t] > 0, meta[0, t], trash)
        product = dot(terms[source], held[t], NN)
        half = product.shape[0] // 2
        total[target] += product[:half] + product[half:]
    for i, out in enumerate(outs):
        out[...] = total[i * blocks : (i + 1) * blocks]


def forward_kernel(meta, held, kept_ref, *rest):
    sources, out, (terms, total) = rest[ROUNDS::-1], rest[ROUNDS + 1], rest[-2:]
    blocks = kept_ref.shape[0]
    trash = blocks
    for i, ref in enumerate(sources):
        for b in range(blocks):
            terms[i * blocks + b] = split(ref[b])
    total[:blocks] = kept_ref[...]
    total[trash] = jnp.zeros(total.shape[1:], F32)
    for t in range(held.shape[0]):
        source = meta[0, t]
        target = jnp.where(meta[2, t] > 0, meta[1, t], trash)
        product = dot(terms[source], held[t], NT)
        half = product.shape[0] // 2
        total[target] += product[:half] + product[half:]
    out[...] = total[:blocks]


def rep_sum_kernel(second, first, third, own, out):
    n = own.shape[0]
    for b in range(n):
        out[b] = (own[b] + second[(b - 2) % n]) + (first[(b - 1) % n] + third[(b - 3) % n])


def gram_kernel(second, first, third, own, s_ref, y_ref, z_own, out):
    blocks, k, width = s_ref.shape
    grams = []
    for b in range(blocks):
        z = (own[b] + second[(b - 2) % blocks]) + (first[(b - 1) % blocks] + third[(b - 3) % blocks])
        if b == 0:
            z_own[0] = z
        stack = jnp.concatenate([s_ref[b], y_ref[b], z, jnp.zeros((k, width), F32)], axis=0)
        grams.append(dot(stack[: 3 * k], stack, NT, HIGHEST))
    half = blocks // 2
    pairs = [grams[i] + grams[i + half] for i in range(half)]
    gram = functools.reduce(lambda a, b: a + b, pairs)
    out[:k] = jnp.concatenate([gram[:k, : 3 * k], gram[2 * k :, 2 * k : 3 * k]], axis=1)
    rows = k // 2
    cut = [gram[k + i * rows : k + (i + 1) * rows, k : 3 * k] for i in range(2)]
    out[k:] = jnp.concatenate(cut, axis=1)


def tail_kernel(gram_ref, s_ref, y_ref, z_ref, next_ref, coef_ref, fact_ref, upper, inverse):
    lanes, w = gram_ref.shape[1], 8
    k = lanes // 4
    n = 3 * k
    shape = (w, lanes)
    lane = lax.broadcasted_iota(jnp.int32, shape, 1)
    main, below = gram_ref[:k, :], gram_ref[k:, :]
    sy, sz, zz = main[:, k : 2 * k], main[:, 2 * k : 3 * k], main[:, 3 * k :]
    cut = jnp.concatenate([below[:, : 2 * k], below[:, 2 * k :]], axis=0)
    yz = cut[:, k:]
    zero = jnp.zeros((k, k), F32)
    upper[:k] = main
    upper[k : 2 * k] = jnp.concatenate([sy.T, cut, zero], axis=1)
    upper[2 * k :] = jnp.concatenate([sz.T, yz.T, zz, zero], axis=1)
    held = [upper[i * w : (i + 1) * w, :] for i in range(n // w)]
    for i in range(k // w):
        held[i] = jnp.where(lane < n, held[i], 0.0)

    def spread(x):
        return jnp.broadcast_to(x, shape)

    for j in range(n // w):
        at = j * w
        if at == 2 * k:
            x11, x22 = inverse[:k, :k], inverse[k : 2 * k, k : 2 * k]
            u12, u13 = upper[:k, k : 2 * k], upper[:k, 2 * k : n]
            u22, u23 = upper[k : 2 * k, k : 2 * k], upper[k : 2 * k, 2 * k : n]
            fact_ref[0] = dot(x11, u22, NT, HIGHEST)
            coef_ref[0, :, :k] = dot(x11, u12, NT, HIGHEST)
            coef_ref[0, :, k:] = jnp.zeros((k, k), F32)
            v = dot(x11, u12, TN, HIGHEST)
            coef_ref[1, :, :k] = dot(x22, u23 - dot(u22, v, NN, HIGHEST), NT, HIGHEST)
            coef_ref[1, :, k:] = dot(x22, u13 - dot(u12, v, NN, HIGHEST), NT, HIGHEST)
        inside = (lane >= at) & (lane < at + w)
        columns = [spread(held[j][:, at + c : at + c + 1]) for c in range(w)]
        p = [[spread(columns[b][a : a + 1, :]) if a <= b else None for b in range(w)] for a in range(w)]
        rows = [
            jnp.where(inside, jnp.where(lane == at + a, 1.0, 0.0), spread(held[j][a : a + 1, :]))
            for a in range(w)
        ]
        inv, m = [], [[None] * w for _ in range(w)]
        for c in range(w):
            inv.append(1.0 / p[c][c])
            for a in range(c + 1, w):
                m[a][c] = p[c][a] * inv[c]
                for b in range(a, w):
                    p[a][b] = p[a][b] - m[a][c] * p[c][b]
                rows[a] = rows[a] - m[a][c] * rows[c]
        for i in range(j + 1, n // w):
            f = []
            for c in range(w):
                value = spread(held[i][:, at + c : at + c + 1])
                for d in range(c):
                    value = value - f[d] * m[c][d]
                f.append(value)
            new = jnp.where(inside, 0.0, held[i])
            for c in range(w):
                new = new - (f[c] * inv[c]) * rows[c]
            held[i] = new
        for a in range(w):
            root = lax.rsqrt(p[a][a])
            row = rows[a] * root
            diag = jnp.zeros(shape, F32)
            for b in range(a, w):
                diag = jnp.where(lane == at + b, p[a][b], diag)
            inverse[at + a : at + a + 1, :] = jnp.where(lane < at + w, row, 0.0)[:1]
            upper[at + a : at + a + 1, :] = jnp.where(lane >= at + w, row, diag * root)[:1]
    fact_ref[1] = dot(x22, upper[2 * k :, 2 * k : n], NT, HIGHEST)
    stack = jnp.concatenate([s_ref[0], y_ref[0], z_ref[0]], axis=0)
    next_ref[...] = dot(inverse[2 * k :, :n], stack, NN, HIGHEST)


def moved(x, axis, target):
    size = lax.axis_size(axis)
    return lax.ppermute(x, axis, [(i, target(i) % size) for i in range(size)])


def shifted(x, axis, by):
    return moved(x, axis, lambda i: i + by)


def sum_of_ring(x, ring):
    first, second, third = ring(1), ring(2), ring(3)
    return (x + second) + (first + third)


def body(tiles, tile_row, tile_col, tile_round, tile_count, start_block):
    tiles = tiles[0, 0]
    slots, edge = tiles.shape[0], tiles.shape[1]
    k = start_block.shape[0]
    members = lax.axis_size("rep")
    devices = lax.axis_size("rows")
    blocks = members
    offsets = [max(1, devices // 2**r) for r in range(1, ROUNDS + 1)]
    held_shape = (blocks, k, edge)
    smem = pl.BlockSpec(memory_space=pltpu.SMEM)
    vmem = pl.BlockSpec(memory_space=pltpu.VMEM)
    block_shape = jax.ShapeDtypeStruct(held_shape, F32)
    params = pltpu.CompilerParams(vmem_limit_bytes=VMEM_LIMIT)
    cost = pl.CostEstimate(
        flops=4 * slots * edge * edge * k, bytes_accessed=2 * slots * edge * edge, transcendentals=0
    )

    def scratch(sources, targets):
        return [pltpu.VMEM((sources, 2 * k, edge), BF16), pltpu.VMEM((targets + 1, k, edge), F32)]

    member = lax.axis_index("rep")
    column = lax.rem(member - tile_col[0, 0] + blocks, blocks)
    row = lax.rem(member - tile_row[0, 0] + blocks, blocks)
    live = (jnp.arange(slots, dtype=jnp.int32) < tile_count[0]).astype(jnp.int32)
    meta = jnp.stack([(tile_round[0, 0] * blocks + column) * live, row * live, live], 0)
    own = pl.pallas_call(
        ready_kernel,
        out_shape=jax.ShapeDtypeStruct(start_block.shape, F32),
        in_specs=[vmem, vmem],
        out_specs=vmem,
        compiler_params=params,
    )(tiles, start_block)
    backward = pl.pallas_call(
        backward_kernel,
        out_shape=[block_shape] * (ROUNDS + 1),
        in_specs=[smem, vmem, vmem],
        out_specs=[vmem] * (ROUNDS + 1),
        scratch_shapes=scratch(blocks, (ROUNDS + 1) * blocks),
        compiler_params=params,
        cost_estimate=cost,
    )
    forward = pl.pallas_call(
        forward_kernel,
        out_shape=block_shape,
        in_specs=[smem] + [vmem] * (ROUNDS + 3),
        out_specs=vmem,
        scratch_shapes=scratch((ROUNDS + 1) * blocks, blocks),
        compiler_params=params,
        cost_estimate=cost,
    )

    def rep_parts(part):
        return *[shifted(part, "rep", by) for by in (2, 1, 3)], part

    def rep_sum(part):
        return pl.pallas_call(
            rep_sum_kernel,
            out_shape=block_shape,
            in_specs=[vmem] * 4,
            out_specs=vmem,
            compiler_params=params,
        )(*rep_parts(part))

    def apply(q):
        _, quarter, _, last = offsets
        kept, out32, out16, out8, out4 = backward(meta, tiles, q)
        got4 = shifted(q, "rows", -last)
        got16 = shifted(q, "rows", -quarter)
        u = shifted(out8, "rows", last)
        w = shifted(out32, "rows", quarter)
        got8 = shifted(got4, "rows", -last)
        got32 = shifted(got16, "rows", -quarter)
        v = shifted(out4 + u, "rows", last)
        x = shifted(out16 + w, "rows", quarter)
        part = forward(meta, tiles, kept, got4, got8, got16, got32, q)
        return part + v + x

    start = jnp.stack([own] + [shifted(start_block, "rep", by) for by in range(1, members)], 0)
    first = rep_sum(apply(start))
    second, gram = pl.pallas_call(
        gram_kernel,
        out_shape=[
            jax.ShapeDtypeStruct((1, k, edge), F32),
            jax.ShapeDtypeStruct((k + k // 2, 4 * k), F32),
        ],
        in_specs=[vmem] * 6,
        out_specs=[vmem] * 2,
        compiler_params=params,
    )(*rep_parts(apply(first)), start, first)
    gram = gram + moved(gram, "rows", lambda i: i ^ 1)
    gram = sum_of_ring(gram, lambda by: shifted(gram, "rows", by * (devices // 4)))
    def along_z(by):
        return moved(gram, "rows", lambda i: (i & ~14) | ((i + (2 * by if i & 1 else -2 * by)) & 14))

    near, middle, far, opposite = along_z(1), along_z(2), along_z(3), along_z(4)
    near2, middle2, far2 = [moved(x, "rows", lambda i: i ^ 1) for x in (near, middle, far)]
    gram = ((gram + opposite) + (middle + middle2)) + ((near + far2) + (far + near2))
    result, coefficients, factors = pl.pallas_call(
        tail_kernel,
        out_shape=[
            jax.ShapeDtypeStruct((k, edge), F32),
            jax.ShapeDtypeStruct((2, k, 2 * k), F32),
            jax.ShapeDtypeStruct((2, k, k), F32),
        ],
        in_specs=[vmem] * 4,
        out_specs=[vmem] * 3,
        scratch_shapes=[pltpu.VMEM((3 * k, 4 * k), F32), pltpu.VMEM((3 * k, 4 * k), F32)],
        compiler_params=params,
    )(gram, start, first, second)
    return result, jnp.swapaxes(coefficients, 1, 2), factors


def solution(mesh):
    placed = (
        P("rows", "rep", None, None, None),
        P("rows", "rep", None),
        P("rows", "rep", None),
        P("rows", "rep", None),
        P("rows", "rep"),
        P(None, ("rows", "rep")),
    )
    return jax.shard_map(
        body,
        mesh=mesh,
        in_specs=placed,
        out_specs=(P(None, ("rows", "rep")), P(), P()),
        check_vma=False,
    )
```

```python
import functools

import jax
import jax.numpy as jnp
from jax import lax
from jax.experimental import pallas as pl
from jax.experimental.pallas import tpu as pltpu
from jax.sharding import PartitionSpec as P

ROUNDS = 4
F32 = jnp.float32
BF16 = jnp.bfloat16
HIGHEST = lax.Precision.HIGHEST
VMEM_LIMIT = 40 * 1024 * 1024


def dot(a, b, dims, precision=None):
    return lax.dot_general(a, b, (dims, ((), ())), precision=precision, preferred_element_type=F32)


NN = ((1,), (0,))
NT = ((1,), (1,))
TN = ((0,), (0,))


def split(x):
    high = x.astype(BF16)
    low = (x - high.astype(F32)).astype(BF16)
    return jnp.concatenate([high, low], axis=0)


def ready_kernel(tiles_ref, start_ref, start_out):
    start_out[...] = start_ref[...]


def backward_kernel(meta, held, q_ref, *rest):
    outs, (terms, total) = rest[:-2], rest[-2:]
    blocks = q_ref.shape[0]
    trash = total.shape[0] - 1
    for b in range(blocks):
        terms[b] = split(q_ref[b])
    total[...] = jnp.zeros_like(total)
    for t in range(held.shape[0]):
        source = meta[1, t]
        target = jnp.where(meta[2, t] > 0, meta[0, t], trash)
        product = dot(terms[source], held[t], NN)
        half = product.shape[0] // 2
        total[target] += product[:half] + product[half:]
    for i, out in enumerate(outs):
        out[...] = total[i * blocks : (i + 1) * blocks]


def forward_kernel(meta, held, kept_ref, *rest):
    sources, out, (terms, total) = rest[ROUNDS::-1], rest[ROUNDS + 1], rest[-2:]
    blocks = kept_ref.shape[0]
    trash = blocks
    for i, ref in enumerate(sources):
        for b in range(blocks):
            terms[i * blocks + b] = split(ref[b])
    total[:blocks] = kept_ref[...]
    total[trash] = jnp.zeros(total.shape[1:], F32)
    for t in range(held.shape[0]):
        source = meta[0, t]
        target = jnp.where(meta[2, t] > 0, meta[1, t], trash)
        product = dot(terms[source], held[t], NT)
        half = product.shape[0] // 2
        total[target] += product[:half] + product[half:]
    out[...] = total[:blocks]


def rep_sum_kernel(second, first, third, own, out):
    n = own.shape[0]
    for b in range(n):
        out[b] = (own[b] + second[(b - 2) % n]) + (first[(b - 1) % n] + third[(b - 3) % n])


def gram_kernel(second, first, third, own, s_ref, y_ref, z_own, out):
    blocks, k, width = s_ref.shape
    grams = []
    for b in range(blocks):
        z = (own[b] + second[(b - 2) % blocks]) + (first[(b - 1) % blocks] + third[(b - 3) % blocks])
        if b == 0:
            z_own[0] = z
        stack = jnp.concatenate([s_ref[b], y_ref[b], z, jnp.zeros((k, width), F32)], axis=0)
        grams.append(dot(stack[: 3 * k], stack, NT, HIGHEST))
    half = blocks // 2
    pairs = [grams[i] + grams[i + half] for i in range(half)]
    gram = functools.reduce(lambda a, b: a + b, pairs)
    out[:k] = jnp.concatenate([gram[:k, : 3 * k], gram[2 * k :, 2 * k : 3 * k]], axis=1)
    rows = k // 2
    cut = [gram[k + i * rows : k + (i + 1) * rows, k : 3 * k] for i in range(2)]
    out[k:] = jnp.concatenate(cut, axis=1)


def tail_kernel(gram_ref, s_ref, y_ref, z_ref, next_ref, coef_ref, fact_ref, upper, inverse):
    lanes, w = gram_ref.shape[1], 8
    k = lanes // 4
    n = 3 * k
    shape = (w, lanes)
    lane = lax.broadcasted_iota(jnp.int32, shape, 1)
    main, below = gram_ref[:k, :], gram_ref[k:, :]
    sy, sz, zz = main[:, k : 2 * k], main[:, 2 * k : 3 * k], main[:, 3 * k :]
    cut = jnp.concatenate([below[:, : 2 * k], below[:, 2 * k :]], axis=0)
    yz = cut[:, k:]
    zero = jnp.zeros((k, k), F32)
    upper[:k] = main
    upper[k : 2 * k] = jnp.concatenate([sy.T, cut, zero], axis=1)
    upper[2 * k :] = jnp.concatenate([sz.T, yz.T, zz, zero], axis=1)
    held = [upper[i * w : (i + 1) * w, :] for i in range(n // w)]
    for i in range(k // w):
        held[i] = jnp.where(lane < n, held[i], 0.0)

    def spread(x):
        return jnp.broadcast_to(x, shape)

    for j in range(n // w):
        at = j * w
        if at == 2 * k:
            x11, x22 = inverse[:k, :k], inverse[k : 2 * k, k : 2 * k]
            u12, u13 = upper[:k, k : 2 * k], upper[:k, 2 * k : n]
            u22, u23 = upper[k : 2 * k, k : 2 * k], upper[k : 2 * k, 2 * k : n]
            fact_ref[0] = dot(x11, u22, NT, HIGHEST)
            coef_ref[0, :, :k] = dot(x11, u12, NT, HIGHEST)
            coef_ref[0, :, k:] = jnp.zeros((k, k), F32)
            v = dot(x11, u12, TN, HIGHEST)
            coef_ref[1, :, :k] = dot(x22, u23 - dot(u22, v, NN, HIGHEST), NT, HIGHEST)
            coef_ref[1, :, k:] = dot(x22, u13 - dot(u12, v, NN, HIGHEST), NT, HIGHEST)
        inside = (lane >= at) & (lane < at + w)
        columns = [spread(held[j][:, at + c : at + c + 1]) for c in range(w)]
        p = [[spread(columns[b][a : a + 1, :]) if a <= b else None for b in range(w)] for a in range(w)]
        rows = [
            jnp.where(inside, jnp.where(lane == at + a, 1.0, 0.0), spread(held[j][a : a + 1, :]))
            for a in range(w)
        ]
        inv, m = [], [[None] * w for _ in range(w)]
        for c in range(w):
            inv.append(1.0 / p[c][c])
            for a in range(c + 1, w):
                m[a][c] = p[c][a] * inv[c]
                for b in range(a, w):
                    p[a][b] = p[a][b] - m[a][c] * p[c][b]
                rows[a] = rows[a] - m[a][c] * rows[c]
        for i in range(j + 1, n // w):
            f = []
            for c in range(w):
                value = spread(held[i][:, at + c : at + c + 1])
                for d in range(c):
                    value = value - f[d] * m[c][d]
                f.append(value)
            new = jnp.where(inside, 0.0, held[i])
            for c in range(w):
                new = new - (f[c] * inv[c]) * rows[c]
            held[i] = new
        for a in range(w):
            root = lax.rsqrt(p[a][a])
            row = rows[a] * root
            diag = jnp.zeros(shape, F32)
            for b in range(a, w):
                diag = jnp.where(lane == at + b, p[a][b], diag)
            inverse[at + a : at + a + 1, :] = jnp.where(lane < at + w, row, 0.0)[:1]
            upper[at + a : at + a + 1, :] = jnp.where(lane >= at + w, row, diag * root)[:1]
    fact_ref[1] = dot(x22, upper[2 * k :, 2 * k : n], NT, HIGHEST)
    stack = jnp.concatenate([s_ref[0], y_ref[0], z_ref[0]], axis=0)
    next_ref[...] = dot(inverse[2 * k :, :n], stack, NN, HIGHEST)


def moved(x, axis, target):
    size = lax.axis_size(axis)
    return lax.ppermute(x, axis, [(i, target(i) % size) for i in range(size)])


def shifted(x, axis, by):
    return moved(x, axis, lambda i: i + by)


def sum_of_ring(x, ring):
    first, second, third = ring(1), ring(2), ring(3)
    return (x + second) + (first + third)


def body(tiles, tile_row, tile_col, tile_round, tile_count, start_block):
    tiles = tiles[0, 0]
    slots, edge = tiles.shape[0], tiles.shape[1]
    k = start_block.shape[0]
    members = lax.axis_size("rep")
    devices = lax.axis_size("rows")
    blocks = members
    offsets = [max(1, devices // 2**r) for r in range(1, ROUNDS + 1)]
    held_shape = (blocks, k, edge)
    smem = pl.BlockSpec(memory_space=pltpu.SMEM)
    vmem = pl.BlockSpec(memory_space=pltpu.VMEM)
    block_shape = jax.ShapeDtypeStruct(held_shape, F32)
    params = pltpu.CompilerParams(vmem_limit_bytes=VMEM_LIMIT)
    cost = pl.CostEstimate(
        flops=4 * slots * edge * edge * k, bytes_accessed=2 * slots * edge * edge, transcendentals=0
    )

    def scratch(sources, targets):
        return [pltpu.VMEM((sources, 2 * k, edge), BF16), pltpu.VMEM((targets + 1, k, edge), F32)]

    own = pl.pallas_call(
        ready_kernel,
        out_shape=jax.ShapeDtypeStruct(start_block.shape, F32),
        in_specs=[vmem, vmem],
        out_specs=vmem,
        compiler_params=params,
    )(tiles, start_block)
    start = jnp.stack([own] + [shifted(start_block, "rep", by) for by in range(1, members)], 0)
    tile_row, tile_col, tile_round, tile_count, _ = lax.optimization_barrier(
        (tile_row, tile_col, tile_round, tile_count, start)
    )
    member = lax.axis_index("rep")
    column = lax.rem(member - tile_col[0, 0] + blocks, blocks)
    row = lax.rem(member - tile_row[0, 0] + blocks, blocks)
    live = (jnp.arange(slots, dtype=jnp.int32) < tile_count[0]).astype(jnp.int32)
    meta = jnp.stack([(tile_round[0, 0] * blocks + column) * live, row * live, live], 0)
    backward = pl.pallas_call(
        backward_kernel,
        out_shape=[block_shape] * (ROUNDS + 1),
        in_specs=[smem, vmem, vmem],
        out_specs=[vmem] * (ROUNDS + 1),
        scratch_shapes=scratch(blocks, (ROUNDS + 1) * blocks),
        compiler_params=params,
        cost_estimate=cost,
    )
    forward = pl.pallas_call(
        forward_kernel,
        out_shape=block_shape,
        in_specs=[smem] + [vmem] * (ROUNDS + 3),
        out_specs=vmem,
        scratch_shapes=scratch((ROUNDS + 1) * blocks, blocks),
        compiler_params=params,
        cost_estimate=cost,
    )

    def rep_parts(part):
        return *[shifted(part, "rep", by) for by in (2, 1, 3)], part

    def rep_sum(part):
        return pl.pallas_call(
            rep_sum_kernel,
            out_shape=block_shape,
            in_specs=[vmem] * 4,
            out_specs=vmem,
            compiler_params=params,
        )(*rep_parts(part))

    def apply(q):
        _, quarter, _, last = offsets
        kept, out32, out16, out8, out4 = backward(meta, tiles, q)
        got4 = shifted(q, "rows", -last)
        got16 = shifted(q, "rows", -quarter)
        u = shifted(out8, "rows", last)
        w = shifted(out32, "rows", quarter)
        got8 = shifted(got4, "rows", -last)
        got32 = shifted(got16, "rows", -quarter)
        v = shifted(out4 + u, "rows", last)
        x = shifted(out16 + w, "rows", quarter)
        part = forward(meta, tiles, kept, got4, got8, got16, got32, q)
        return part + v + x

    first = rep_sum(apply(start))
    second, gram = pl.pallas_call(
        gram_kernel,
        out_shape=[
            jax.ShapeDtypeStruct((1, k, edge), F32),
            jax.ShapeDtypeStruct((k + k // 2, 4 * k), F32),
        ],
        in_specs=[vmem] * 6,
        out_specs=[vmem] * 2,
        compiler_params=params,
    )(*rep_parts(apply(first)), start, first)
    gram = gram + moved(gram, "rows", lambda i: i ^ 1)
    gram = sum_of_ring(gram, lambda by: shifted(gram, "rows", by * (devices // 4)))
    def along_z(by):
        return moved(gram, "rows", lambda i: (i & ~14) | ((i + (2 * by if i & 1 else -2 * by)) & 14))

    near, middle, far, opposite = along_z(1), along_z(2), along_z(3), along_z(4)
    near2, middle2, far2 = [moved(x, "rows", lambda i: i ^ 1) for x in (near, middle, far)]
    gram = ((gram + opposite) + (middle + middle2)) + ((near + far2) + (far + near2))
    result, coefficients, factors = pl.pallas_call(
        tail_kernel,
        out_shape=[
            jax.ShapeDtypeStruct((k, edge), F32),
            jax.ShapeDtypeStruct((2, k, 2 * k), F32),
            jax.ShapeDtypeStruct((2, k, k), F32),
        ],
        in_specs=[vmem] * 4,
        out_specs=[vmem] * 3,
        scratch_shapes=[pltpu.VMEM((3 * k, 4 * k), F32), pltpu.VMEM((3 * k, 4 * k), F32)],
        compiler_params=params,
    )(gram, start, first, second)
    return result, jnp.swapaxes(coefficients, 1, 2), factors


def solution(mesh):
    placed = (
        P("rows", "rep", None, None, None),
        P("rows", "rep", None),
        P("rows", "rep", None),
        P("rows", "rep", None),
        P("rows", "rep"),
        P(None, ("rows", "rep")),
    )
    return jax.shard_map(
        body,
        mesh=mesh,
        in_specs=placed,
        out_specs=(P(None, ("rows", "rep")), P(), P()),
        check_vma=False,
    )
```
